32 devices in a mesh: lat: 4 (over y, core), lon: 8 (over z, x).
Axes of the slice: x: 2, y: 2, z: 4, core: 2. Of those that a mesh axis runs over, the one named last changes fastest.
Arguments:
- observation_residual: bfloat16 [128, 16384], P(None, ('lat', 'lon')), may hold values from -6 to 6
- obs_index: int32 [2, 16384], P(None, ('lat', 'lon')), may hold values from 0 to 8191, as said below
- obs_count: int32 [1, 1024], P(None, ('lat', 'lon')), may hold values from 12 to 16, as said below
- obs_weight: float32 [128], replicated, may hold values from 0.3 to 3
- jacobian: bfloat16 [128, 8, 137], replicated, may hold values from -0.5 to 0.5
- decoder: bfloat16 [137, 128], replicated, may hold values from -0.5 to 0.5
- conv_weight: bfloat16 [4, 3, 128, 128], replicated, may hold values from -0.3125 to 0.3125
- gates: bfloat16 [4, 128, 512, 512], P(None, None, 'lon', 'lat'), may hold values from 0.049804688 to 1.09375
- encoder: bfloat16 [128, 137], replicated, may hold values from -0.5 to 0.5
Outputs:
- state_grad: float32 [137, 512, 512], P(None, 'lon', 'lat')
The draws below stay inside these ranges and needn't reach their ends.
Inputs may be any that keep to these rules, and one draw needn't show every extreme that they name: `obs_index`: row 0 is a column within the destination tile, longitude offset * 128 + latitude offset, up to 8191; row 1 is a Jacobian block below 8. `obs_count`: slots of a pair at or after its count are unused. In every draw some tiles receive 16 from every sender.
All inputs are finite; a program needn't handle non-finite values.
Results may differ from the reference program's by a relative error of at most 0.0056.
Values may be sent and summed in bfloat16 or wider, within the bound.
A program may use at most 128 MiB of HBM per device.

```python
import math
import jax
import jax.numpy as jnp
from jax import lax

C = 128
CH = 128
LEV = 137
NCLASS = 8
LAYERS = 4
TLAT = 128
TLON = 64
SLOT = 16
CELLS = 8192
NLAT = 512
NLON = 512
NOBS = 16384
N_LAT = 4
N_LON = 8
DEVICES = 32


def draw_obs_count(key, part):
    key_order = jax.random.fold_in(key, 11)
    key_light = jax.random.fold_in(key, 12)
    heavy_count = max(1, DEVICES // 16)
    order = jax.random.permutation(key_order, DEVICES)
    heavy = order < heavy_count
    lowest = SLOT - max(1, SLOT // 4)
    light = jax.random.randint(key_light, (DEVICES, DEVICES), lowest, SLOT + 1)
    counts = jnp.where(heavy[None, :], SLOT, light)
    return counts.reshape(1, DEVICES * DEVICES).astype(jnp.int32)


def draw_obs_index(key, part):
    key_cells = jax.random.fold_in(key, 21)
    key_kinds = jax.random.fold_in(key, 22)
    key_place = jax.random.fold_in(key, 23)
    cells = jax.random.randint(key_cells, (NOBS,), 0, CELLS)
    place = jax.random.randint(key_place, (), 0, NOBS)
    cells = cells.at[place].set(CELLS - 1)
    kinds = jax.random.randint(key_kinds, (NOBS,), 0, NCLASS)
    return jnp.stack([cells, kinds]).astype(jnp.int32)


def block_scale(own_key, dims, pieces, smallest, high):
    loudness = 1.0
    for dim, blocks in pieces:
        draws = jax.random.uniform(jax.random.fold_in(jax.random.fold_in(own_key, 6), dim), (blocks,), jnp.float32, smallest / len(pieces), high / len(pieces))
        loudness = loudness * jnp.repeat(jnp.exp(draws), dims[dim] // blocks).reshape((-1,) + (1,) * (len(dims) - 1 - dim))
    return loudness


def bell_draw(stream_key, dims, scale, most, split=(), kind=jnp.bfloat16):
    drawn = jax.random.normal(stream_key, dims, jnp.float32) * scale
    if len(split) > 0:
        drawn = block_scale(stream_key, dims, split, -0.22, 0.18) * drawn
    return jnp.clip(drawn, min=-most, max=most).astype(kind)


def setup_inputs(seed: int = 0) -> dict:
    splits = jax.random.split(jax.random.key(seed), 10)
    return {
        "observation_residual": bell_draw(splits[0], (CH, NOBS), 1.0, 6.0, ((1, 32),)),
        "obs_index": draw_obs_index(jax.random.fold_in(splits[9], 71), 0),
        "obs_count": draw_obs_count(jax.random.fold_in(splits[9], 71), 0),
        "obs_weight": jnp.clip(jnp.exp(jax.random.uniform(splits[3], (CH,), jnp.float32, math.log(0.3), math.log(3.0))), 0.3, 3.0),
        "jacobian": bell_draw(splits[4], (CH, NCLASS, LEV), CH ** -0.5, 0.5),
        "decoder": bell_draw(splits[5], (LEV, C), C ** -0.5, 0.5),
        "conv_weight": bell_draw(splits[6], (LAYERS, 3, C, C), (3 * C) ** -0.5, 0.3125),
        "gates": jnp.clip(0.049804688 + 1.0439453 * jax.random.uniform(splits[7], (LAYERS, C, NLON, NLAT), jnp.float32) ** block_scale(splits[7], (LAYERS, C, NLON, NLAT), ((2, 8), (3, 4)), -0.2, 0.2), 0.049804688, 1.09375).astype(jnp.bfloat16),
        "encoder": bell_draw(splits[8], (C, LEV), LEV ** -0.5, 0.5),
    }


def rounded(value):
    return lax.optimization_barrier(value.astype(jnp.bfloat16)).astype(jnp.float32)


def reference(observation_residual, obs_index, obs_count, obs_weight, jacobian, decoder, conv_weight, gates, encoder):
    device_count = N_LAT * N_LON
    nobs = observation_residual.shape[1]
    position = jnp.arange(nobs, dtype=jnp.int32)
    pair = position // SLOT
    valid = (position % SLOT) < obs_count[0][pair]
    weighted = rounded(jnp.where(valid[None, :], obs_weight[:, None] * observation_residual.astype(jnp.float32), 0.0))
    kinds = obs_index[1]
    incr = jnp.zeros((LEV, nobs), jnp.float32)
    for kind in range(NCLASS):
        part_incr = jnp.dot(jacobian[:, kind, :].astype(jnp.float32).T, weighted)
        incr = jnp.where(kinds[None, :] == kind, part_incr, incr)
    incr = rounded(incr)
    dest = pair % device_count
    lat_tile = dest // N_LON
    lon_tile = dest % N_LON
    cell = obs_index[0]
    lon_glob = lon_tile * TLON + cell // TLAT
    lat_glob = lat_tile * TLAT + cell % TLAT
    flat = (lon_glob * NLAT + lat_glob).astype(jnp.int32)
    column_grad = jnp.zeros((LEV, NLON * NLAT), jnp.float32).at[:, flat].add(incr)
    hidden = jnp.dot(decoder.astype(jnp.float32).T, rounded(column_grad))
    for layer in reversed(range(LAYERS)):
        field = rounded(hidden).reshape(C, NLON, NLAT)
        back = jnp.zeros((C, NLON * NLAT), jnp.float32)
        for tap in range(3):
            moved = jnp.roll(field, 4 * (tap - 1), axis=1).reshape(C, -1)
            back = back + jnp.dot(conv_weight[layer, tap].astype(jnp.float32).T, moved)
        hidden = hidden + gates[layer].astype(jnp.float32).reshape(C, -1) * back
    state_grad = column_grad + jnp.dot(encoder.astype(jnp.float32).T, rounded(hidden))
    return state_grad.reshape(LEV, NLON, NLAT)
```

```python
import functools

import jax
import jax.numpy as jnp
from jax import lax
from jax.experimental import pallas as pl
from jax.experimental.pallas import tpu as pltpu
from jax.sharding import PartitionSpec as P

MESH = pl.DeviceIdType.MESH
F32 = jnp.float32
BF16 = jnp.bfloat16


def up(value, unit):
    return (value + unit - 1) // unit * unit


def kernel(
    dims,
    resid, index, counts, weight, jac, dec, conv, enc, gates, out,
    sent, got, incr, place, cg, hid, field, stage, gate, taps, dec_t, enc_t, tall, wide, done,
    a2a_send, a2a_recv, halo_send, halo_recv, gate_sem, out_sem,
):
    lat_n, lon_n, slot, kinds_n, levels, layers, width, tile_lon, tile_lat = dims
    devices = lat_n * lon_n
    lev = incr.shape[0]
    quads = tile_lon // 4
    my_lat, my_lon = lax.axis_index("lat"), lax.axis_index("lon")
    me = my_lat * lon_n + my_lon
    right, left = lax.rem(my_lon + 1, lon_n), lax.rem(my_lon + lon_n - 1, lon_n)

    def gate_copy(layer):
        return pltpu.make_async_copy(gates.at[layer], stage.at[layer % 2], gate_sem.at[layer % 2])

    order = list(reversed(range(layers)))
    for layer in order[:2]:
        gate_copy(layer).start()

    barrier = pltpu.get_barrier_semaphore()

    @pl.loop(1, devices)
    def _(off):
        d = lax.rem(me + off, devices)
        pl.semaphore_signal(
            barrier, inc=1, device_id=(d // lon_n, lax.rem(d, lon_n)), device_id_type=MESH
        )

    weight_lanes = jnp.transpose(jnp.broadcast_to(weight[...], (128, weight.shape[1])))
    counts8 = jnp.broadcast_to(counts[...].astype(F32), (8, devices)).astype(BF16)

    @pl.loop(0, devices * slot // 128)
    def _(chunk):
        lanes = pl.ds(pl.multiple_of(chunk * 128, 128), 128)
        pair = (lax.broadcasted_iota(jnp.int32, (devices, 128), 1) + chunk * 128) // slot
        owner = lax.broadcasted_iota(jnp.int32, (devices, 128), 0)
        spread = jnp.where(pair == owner, 1.0, 0.0).astype(BF16)
        limit = jnp.dot(counts8, spread, preferred_element_type=F32)[0:1]
        nth = lax.broadcasted_iota(jnp.int32, (1, 128), 1) % slot
        used = nth.astype(F32) < limit
        weighted = jnp.where(used, weight_lanes * resid[:, lanes].astype(F32), 0.0)
        kinds = index[1:2, lanes]
        cells = index[0:1, lanes]
        rows = [
            jnp.where(kinds == k, weighted, 0.0).astype(BF16) for k in range(kinds_n)
        ]
        row = lax.broadcasted_iota(jnp.int32, (16, 128), 0)
        lon = (cells // tile_lat).astype(F32)
        lat = (cells % tile_lat).astype(F32)
        rows.append(jnp.where(row == 0, lon, jnp.where(row == 1, lat, 0.0)).astype(BF16))
        stack = jnp.concatenate(rows, axis=0)
        sent[lanes, :] = lax.dot_general(
            stack, jac[...], (((0,), (0,)), ((), ())), preferred_element_type=F32
        ).astype(BF16)

    pl.semaphore_wait(barrier, devices - 1)

    mine = pl.ds(pl.multiple_of(me * slot, slot), slot)

    def slots_to(d):
        return pltpu.make_async_remote_copy(
            src_ref=sent.at[pl.ds(pl.multiple_of(d * slot, slot), slot)],
            dst_ref=got.at[mine],
            send_sem=a2a_send.at[d],
            recv_sem=a2a_recv.at[me],
            device_id=(d // lon_n, lax.rem(d, lon_n)),
            device_id_type=MESH,
        )

    def slots_from(s):
        return pltpu.make_async_remote_copy(
            src_ref=sent.at[mine],
            dst_ref=got.at[pl.ds(pl.multiple_of(s * slot, slot), slot)],
            send_sem=a2a_send.at[s],
            recv_sem=a2a_recv.at[s],
            device_id=(s // lon_n, lax.rem(s, lon_n)),
            device_id_type=MESH,
        )

    @pl.loop(1, devices)
    def _(off):
        slots_to(lax.rem(me + off, devices)).start()

    got[mine, :] = sent[mine, :]

    for layer in range(layers):
        for tap in range(3):
            taps[layer, :, (2 - tap) * width : (3 - tap) * width] = jnp.transpose(
                conv[layer, tap].astype(F32)
            ).astype(BF16)
    tall[...] = jnp.zeros_like(tall)
    tall[0:levels, :] = dec[...].astype(F32)
    dec_t[...] = jnp.transpose(tall[...])[:, 0:lev].astype(BF16)
    wide[...] = jnp.zeros_like(wide)
    wide[:, 0:levels] = enc[...].astype(F32)
    enc_t[...] = jnp.transpose(wide[...])[0:lev].astype(BF16)

    for at, layer in enumerate(order):
        gate_copy(layer).wait()

        @pl.loop(0, width // 4)
        def _(block):
            for part in range(4):
                c = block * 4 + part
                rows = pl.ds(pl.multiple_of(c * tile_lon, tile_lon), tile_lon)
                gate[layer, rows, :] = stage[layer % 2, c].astype(F32)

        if at + 2 < layers:
            gate_copy(order[at + 2]).start()

    @pl.loop(1, devices)
    def _(off):
        s = lax.rem(me + devices - off, devices)
        slots_from(s).wait_recv()

    @pl.loop(0, devices * slot // 128)
    def _(chunk):
        lanes = pl.ds(pl.multiple_of(chunk * 128, 128), 128)
        block = got[lanes, :].astype(F32)
        incr[:, lanes] = jnp.transpose(block)[0:lev].astype(BF16)
        lane = lax.broadcasted_iota(jnp.int32, (128, tile_lat), 1).astype(F32)
        at_lat = block[:, levels + 1 : levels + 2] == lane
        place[lanes, :] = jnp.where(at_lat, block[:, levels : levels + 1], -1.0).astype(BF16)

    def rows_of(q):
        return pl.ds(pl.multiple_of(q * width, width), width)

    def halos(layer, rp):
        to_right = pltpu.make_async_remote_copy(
            src_ref=field.at[layer, rp, rows_of(quads)],
            dst_ref=field.at[layer, rp, rows_of(0)],
            send_sem=halo_send.at[layer, rp, 0],
            recv_sem=halo_recv.at[layer, rp, 0],
            device_id=(my_lat, right),
            device_id_type=MESH,
        )
        to_left = pltpu.make_async_remote_copy(
            src_ref=field.at[layer, rp, rows_of(1)],
            dst_ref=field.at[layer, rp, rows_of(quads + 1)],
            send_sem=halo_send.at[layer, rp, 1],
            recv_sem=halo_recv.at[layer, rp, 1],
            device_id=(my_lat, left),
            device_id_type=MESH,
        )
        return to_right, to_left

    def scatter(rp, q):
        lon = 4 * (q - 1) + 2 * rp
        hot = []
        for r in range(2):
            value = jnp.full((1, tile_lat), lon + r, jnp.int32).astype(F32).astype(BF16)
            hot.append(jnp.where(place[...] == value, 1.0, 0.0).astype(BF16))
        total = jnp.dot(incr[...], jnp.concatenate(hot, axis=1), preferred_element_type=F32)
        cg[rp, q - 1] = total
        hidden = jnp.dot(dec_t[...], total.astype(BF16), preferred_element_type=F32)
        hid[rp, q - 1] = hidden
        field[layers - 1, rp, rows_of(q), :] = hidden.astype(BF16)

    def conv_at(layer, rp, q):
        window = field[layer, rp, pl.ds(pl.multiple_of((q - 1) * width, width), 3 * width), :]
        back = jnp.dot(taps[layer], window, preferred_element_type=F32)
        lon = 4 * (q - 1) + 2 * rp
        parts = []
        for r in range(2):
            lats = slice(r * tile_lat, (r + 1) * tile_lat)
            factor = gate[layer, pl.ds(lon + r, width, stride=tile_lon), :]
            parts.append(hid[rp, q - 1, :, lats] + factor * back[:, lats])
        return jnp.concatenate(parts, axis=1)

    def step(layer, rp, q):
        hidden = conv_at(layer, rp, q)
        hid[rp, q - 1] = hidden
        field[layer - 1, rp, rows_of(q), :] = hidden.astype(BF16)

    def edges_then_inside(visit, layer):
        for rp in range(2):
            visit(rp, 1)
            visit(rp, quads)
            for copy in halos(layer, rp):
                copy.start()

        @pl.loop(2, quads)
        def _(q):
            for rp in range(2):
                visit(rp, q)

    edges_then_inside(scatter, layers - 1)
    for layer in reversed(range(1, layers)):
        for rp in range(2):
            for copy in halos(layer, rp):
                copy.wait_recv()
        edges_then_inside(functools.partial(step, layer), layer - 1)

    def finish(pair):
        rows = done.at[pair].reshape(lev * 8, tile_lat)
        for half in range(2):
            for rp in range(2):
                q = 2 * pair + half + 1
                hidden = conv_at(0, rp, q).astype(BF16)
                state = cg[rp, q - 1] + jnp.dot(enc_t[...], hidden, preferred_element_type=F32)
                for r in range(2):
                    rows[pl.ds(half * 4 + rp * 2 + r, lev, stride=8), :] = state[
                        :, r * tile_lat : (r + 1) * tile_lat
                    ]
        write(pair).start()

    def write(pair):
        return pltpu.make_async_copy(
            done.at[pair, 0:levels],
            out.at[:, pl.ds(pl.multiple_of(pair * 8, 8), 8), :],
            out_sem.at[pair],
        )

    pairs = quads // 2
    pl.loop(1, pairs - 1)(finish)
    for rp in range(2):
        for copy in halos(0, rp):
            copy.wait_recv()
    finish(0)
    finish(pairs - 1)

    @pl.loop(1, devices)
    def _(off):
        slots_to(lax.rem(me + off, devices)).wait_send()

    for layer in range(layers):
        for rp in range(2):
            for copy in halos(layer, rp):
                copy.wait_send()

    @pl.loop(0, pairs)
    def _(pair):
        write(pair).wait()


def per_device(
    observation_residual, obs_index, obs_count, obs_weight, jacobian, decoder, conv_weight, gates, encoder
):
    lat_n, lon_n = lax.axis_size("lat"), lax.axis_size("lon")
    devices = lat_n * lon_n
    channels, slots = observation_residual.shape
    slot = slots // devices
    kinds_n, levels = jacobian.shape[1:]
    layers, width, tile_lon, tile_lat = gates.shape
    lev = up(levels + 2, 16)
    lanes = up(levels + 2, 128)
    quads = tile_lon // 4

    blocks = jnp.transpose(jacobian, (1, 0, 2)).reshape(kinds_n * channels, levels)
    jac = jnp.pad(blocks, ((0, 16), (0, lanes - levels)))
    row = lax.broadcasted_iota(jnp.int32, jac.shape, 0) - kinds_n * channels
    lane = lax.broadcasted_iota(jnp.int32, jac.shape, 1) - levels
    jac = jnp.where((row >= 0) & (row < 2) & (row == lane), jnp.ones((), BF16), jac)

    dims = (lat_n, lon_n, slot, kinds_n, levels, layers, width, tile_lon, tile_lat)
    vmem = pl.BlockSpec(memory_space=pltpu.VMEM)
    hbm = pl.BlockSpec(memory_space=pl.ANY)
    dma = pltpu.SemaphoreType.DMA
    return pl.pallas_call(
        functools.partial(kernel, dims),
        out_shape=jax.ShapeDtypeStruct((levels, tile_lon, tile_lat), F32),
        in_specs=[vmem] * 8 + [hbm],
        out_specs=hbm,
        scratch_shapes=[
            pltpu.VMEM((slots, lanes), BF16),
            pltpu.VMEM((slots, lanes), BF16),
            pltpu.VMEM((lev, slots), BF16),
            pltpu.VMEM((slots, tile_lat), BF16),
            pltpu.VMEM((2, quads, lev, 2 * tile_lat), F32),
            pltpu.VMEM((2, quads, width, 2 * tile_lat), F32),
            pltpu.VMEM((layers, 2, (quads + 2) * width, 2 * tile_lat), BF16),
            pltpu.VMEM((2, width, tile_lon, tile_lat), BF16),
            pltpu.VMEM((layers, width * tile_lon, tile_lat), F32),
            pltpu.VMEM((layers, width, 3 * width), BF16),
            pltpu.VMEM((width, lev), BF16),
            pltpu.VMEM((lev, width), BF16),
            pltpu.VMEM((lanes, width), F32),
            pltpu.VMEM((width, lanes), F32),
            pltpu.VMEM((quads // 2, lev, 8, tile_lat), F32),
            dma((devices,)),
            dma((devices,)),
            dma((layers, 2, 2)),
            dma((layers, 2, 2)),
            dma((2,)),
            dma((quads // 2,)),
        ],
        compiler_params=pltpu.CompilerParams(
            collective_id=0, has_side_effects=True, vmem_limit_bytes=60 * 1024 * 1024
        ),
    )(
        observation_residual, obs_index, obs_count, obs_weight.reshape(1, channels), jac,
        decoder, conv_weight, encoder, gates,
    )


def solution(mesh):
    return jax.shard_map(
        per_device,
        mesh=mesh,
        in_specs=(
            P(None, ("lat", "lon")),
            P(None, ("lat", "lon")),
            P(None, ("lat", "lon")),
            P(),
            P(),
            P(),
            P(),
            P(None, None, "lon", "lat"),
            P(),
        ),
        out_specs=P(None, "lon", "lat"),
        check_vma=False,
    )
```

```python
import functools

import jax
import jax.numpy as jnp
from jax import lax
from jax.experimental import pallas as pl
from jax.experimental.pallas import tpu as pltpu
from jax.sharding import PartitionSpec as P

MESH = pl.DeviceIdType.MESH
F32 = jnp.float32
BF16 = jnp.bfloat16


def up(value, unit):
    return (value + unit - 1) // unit * unit


def kernel(
    dims,
    resid, index, counts, weight, jac, dec, conv, gates, cg_out, hid_out,
    sent, got, incr, place, cg, hid, last, field, stage, gate, taps, dec_t, tall, blocks, jac_l,
    a2a_send, a2a_recv, halo_send, halo_recv, gate_sem, out_sem,
):
    lat_n, lon_n, slot, kinds_n, levels, layers, width, tile_lon, tile_lat = dims
    devices = lat_n * lon_n
    lev = incr.shape[0]
    quads = tile_lon // 4
    my_lat, my_lon = lax.axis_index("lat"), lax.axis_index("lon")
    me = my_lat * lon_n + my_lon
    right, left = lax.rem(my_lon + 1, lon_n), lax.rem(my_lon + lon_n - 1, lon_n)

    def gate_copy(layer):
        return pltpu.make_async_copy(gates.at[layer], stage.at[layer % 2], gate_sem.at[layer % 2])

    order = list(reversed(range(layers)))
    for layer in order[:2]:
        gate_copy(layer).start()

    barrier = pltpu.get_barrier_semaphore()

    @pl.loop(1, devices)
    def _(off):
        d = lax.rem(me + off, devices)
        pl.semaphore_signal(
            barrier, inc=1, device_id=(d // lon_n, lax.rem(d, lon_n)), device_id_type=MESH
        )

    channels = resid.shape[0]
    blocks[...] = jnp.zeros_like(blocks)
    blocks[0 : levels * kinds_n, :] = jac[...].astype(F32).reshape(levels * kinds_n, -1)
    for k in range(kinds_n):
        jac_l[:, k * channels : (k + 1) * channels] = blocks[pl.ds(k, lev, stride=kinds_n), :].astype(BF16)
    weight_lanes = jnp.transpose(jnp.broadcast_to(weight[...], (128, weight.shape[1])))
    counts8 = jnp.broadcast_to(counts[...].astype(F32), (8, devices)).astype(BF16)
    mine = pl.ds(pl.multiple_of(me * slot, slot), slot)

    def slots_to(d):
        return pltpu.make_async_remote_copy(
            src_ref=sent.at[pl.ds(pl.multiple_of(d * slot, slot), slot)],
            dst_ref=got.at[mine],
            send_sem=a2a_send.at[d],
            recv_sem=a2a_recv.at[me],
            device_id=(d // lon_n, lax.rem(d, lon_n)),
            device_id_type=MESH,
        )

    def slots_from(s):
        return pltpu.make_async_remote_copy(
            src_ref=sent.at[mine],
            dst_ref=got.at[pl.ds(pl.multiple_of(s * slot, slot), slot)],
            send_sem=a2a_send.at[s],
            recv_sem=a2a_recv.at[s],
            device_id=(s // lon_n, lax.rem(s, lon_n)),
            device_id_type=MESH,
        )

    pl.semaphore_wait(barrier, devices - 1)

    chunks = devices * slot // 128
    per_chunk = 128 // slot

    @pl.loop(0, chunks)
    def _(turn):
        chunk = lax.rem(turn + me // per_chunk + 1, chunks)
        lanes = pl.ds(pl.multiple_of(chunk * 128, 128), 128)
        pair = (lax.broadcasted_iota(jnp.int32, (devices, 128), 1) + chunk * 128) // slot
        owner = lax.broadcasted_iota(jnp.int32, (devices, 128), 0)
        spread = jnp.where(pair == owner, 1.0, 0.0).astype(BF16)
        limit = jnp.dot(counts8, spread, preferred_element_type=F32)[0:1]
        nth = lax.broadcasted_iota(jnp.int32, (1, 128), 1) % slot
        used = nth.astype(F32) < limit
        weighted = jnp.where(used, weight_lanes * resid[:, lanes].astype(F32), 0.0)
        kinds = index[1:2, lanes]
        cells = index[0:1, lanes]
        stack = jnp.concatenate(
            [jnp.where(kinds == k, weighted, 0.0).astype(BF16) for k in range(kinds_n)], axis=0
        )
        value = jnp.dot(jac_l[...], stack, preferred_element_type=F32)
        row = lax.broadcasted_iota(jnp.int32, (lev, 128), 0)
        lon = (cells // tile_lat).astype(F32)
        lat = (cells % tile_lat).astype(F32)
        value = jnp.where(row == levels, lon, jnp.where(row == levels + 1, lat, value))
        pad = jnp.zeros((sent.shape[1] - lev, 128), F32)
        sent[lanes, :] = jnp.transpose(jnp.concatenate([value, pad], axis=0)).astype(BF16)

        @pl.loop(0, per_chunk)
        def _(nth):
            d = chunk * per_chunk + lax.rem(nth + me, per_chunk)

            @pl.when(d != me)
            def _():
                slots_to(d).start()

    got[mine, :] = sent[mine, :]

    for layer in range(layers):
        for tap in range(3):
            taps[layer, :, (2 - tap) * width : (3 - tap) * width] = jnp.transpose(
                conv[layer, tap].astype(F32)
            ).astype(BF16)
    tall[...] = jnp.zeros_like(tall)
    tall[0:levels, :] = dec[...].astype(F32)
    dec_t[...] = jnp.transpose(tall[...])[:, 0:lev].astype(BF16)

    for at, layer in enumerate(order):
        gate_copy(layer).wait()

        @pl.loop(0, width // 4)
        def _(block):
            for part in range(4):
                c = block * 4 + part
                rows = pl.ds(pl.multiple_of(c * tile_lon, tile_lon), tile_lon)
                gate[layer, rows, :] = stage[layer % 2, c].astype(F32)

        if at + 2 < layers:
            gate_copy(order[at + 2]).start()

    @pl.loop(1, devices)
    def _(off):
        s = lax.rem(me + devices - off, devices)
        slots_from(s).wait_recv()

    @pl.loop(0, devices * slot // 128)
    def _(chunk):
        lanes = pl.ds(pl.multiple_of(chunk * 128, 128), 128)
        block = got[lanes, :].astype(F32)
        incr[:, lanes] = jnp.transpose(block)[0:lev].astype(BF16)
        lane = lax.broadcasted_iota(jnp.int32, (128, tile_lat), 1).astype(F32)
        at_lat = block[:, levels + 1 : levels + 2] == lane
        place[lanes, :] = jnp.where(at_lat, block[:, levels : levels + 1], -1.0).astype(BF16)

    def rows_of(q):
        return pl.ds(pl.multiple_of(q * width, width), width)

    def halos(layer, rp):
        to_right = pltpu.make_async_remote_copy(
            src_ref=field.at[layer, rp, rows_of(quads)],
            dst_ref=field.at[layer, rp, rows_of(0)],
            send_sem=halo_send.at[layer, rp, 0],
            recv_sem=halo_recv.at[layer, rp, 0],
            device_id=(my_lat, right),
            device_id_type=MESH,
        )
        to_left = pltpu.make_async_remote_copy(
            src_ref=field.at[layer, rp, rows_of(1)],
            dst_ref=field.at[layer, rp, rows_of(quads + 1)],
            send_sem=halo_send.at[layer, rp, 1],
            recv_sem=halo_recv.at[layer, rp, 1],
            device_id=(my_lat, left),
            device_id_type=MESH,
        )
        return to_right, to_left

    def scatter(rp, q):
        lon = 4 * (q - 1) + 2 * rp
        hot = []
        for r in range(2):
            value = jnp.full((1, tile_lat), lon + r, jnp.int32).astype(F32).astype(BF16)
            hot.append(jnp.where(place[...] == value, 1.0, 0.0).astype(BF16))
        total = jnp.dot(incr[...], jnp.concatenate(hot, axis=1), preferred_element_type=F32)
        narrow = total.astype(BF16)
        cg[rp, q - 1] = narrow
        hidden = jnp.dot(dec_t[...], narrow, preferred_element_type=F32)
        hid[rp, q - 1] = hidden
        field[layers - 1, rp, rows_of(q), :] = hidden.astype(BF16)

    def conv_at(layer, rp, q):
        window = field[layer, rp, pl.ds(pl.multiple_of((q - 1) * width, width), 3 * width), :]
        back = jnp.dot(taps[layer], window, preferred_element_type=F32)
        lon = 4 * (q - 1) + 2 * rp
        parts = []
        for r in range(2):
            lats = slice(r * tile_lat, (r + 1) * tile_lat)
            factor = gate[layer, pl.ds(lon + r, width, stride=tile_lon), :]
            parts.append(hid[rp, q - 1, :, lats] + factor * back[:, lats])
        return jnp.concatenate(parts, axis=1)

    def step(layer, rp, q):
        hidden = conv_at(layer, rp, q)
        hid[rp, q - 1] = hidden
        field[layer - 1, rp, rows_of(q), :] = hidden.astype(BF16)

    def edges_then_inside(visit, layer):
        for rp in range(2):
            visit(rp, 1)
            visit(rp, quads)
            for copy in halos(layer, rp):
                copy.start()

        @pl.loop(2, quads)
        def _(q):
            for rp in range(2):
                visit(rp, q)

    edges_then_inside(scatter, layers - 1)
    cg_copy = pltpu.make_async_copy(cg, cg_out, out_sem.at[0])
    cg_copy.start()
    for layer in reversed(range(1, layers)):
        for rp in range(2):
            for copy in halos(layer, rp):
                copy.wait_recv()
        edges_then_inside(functools.partial(step, layer), layer - 1)

    def finish(q):
        for rp in range(2):
            last[rp, q - 1] = conv_at(0, rp, q).astype(BF16)

    def hid_copy(start, count, sem):
        part = pl.ds(start, count)
        return pltpu.make_async_copy(last.at[:, part], hid_out.at[:, part], out_sem.at[sem])

    pl.loop(2, quads)(finish)
    hid_copy(1, quads - 2, 1).start()
    for rp in range(2):
        for copy in halos(0, rp):
            copy.wait_recv()
    finish(1)
    hid_copy(0, 1, 2).start()
    finish(quads)
    hid_copy(quads - 1, 1, 3).start()

    @pl.loop(1, devices)
    def _(off):
        slots_to(lax.rem(me + off, devices)).wait_send()

    for layer in range(layers):
        for rp in range(2):
            for copy in halos(layer, rp):
                copy.wait_send()

    cg_copy.wait()
    hid_copy(1, quads - 2, 1).wait()
    hid_copy(0, 1, 2).wait()
    hid_copy(quads - 1, 1, 3).wait()


def encode_kernel(cg, hid, enc, out):
    levels, lons, tile_lat = out.shape
    rows = out.reshape(levels * lons, tile_lat)
    for half in range(2):
        for rp in range(2):
            state = cg[rp, half, 0:levels].astype(F32) + jnp.dot(
                enc[...], hid[rp, half], preferred_element_type=F32
            )
            for r in range(2):
                rows[pl.ds(half * 4 + rp * 2 + r, levels, stride=lons), :] = state[
                    :, r * tile_lat : (r + 1) * tile_lat
                ]


def per_device(
    observation_residual, obs_index, obs_count, obs_weight, jacobian, decoder, conv_weight, gates, encoder
):
    lat_n, lon_n = lax.axis_size("lat"), lax.axis_size("lon")
    devices = lat_n * lon_n
    channels, slots = observation_residual.shape
    slot = slots // devices
    kinds_n, levels = jacobian.shape[1:]
    layers, width, tile_lon, tile_lat = gates.shape
    lev = up(levels + 2, 16)
    lanes = up(levels + 2, 128)
    quads = tile_lon // 4

    dims = (lat_n, lon_n, slot, kinds_n, levels, layers, width, tile_lon, tile_lat)
    vmem = pl.BlockSpec(memory_space=pltpu.VMEM)
    hbm = pl.BlockSpec(memory_space=pl.ANY)
    dma = pltpu.SemaphoreType.DMA
    cg_shape = (2, quads, lev, 2 * tile_lat)
    hid_shape = (2, quads, width, 2 * tile_lat)
    column_grad, hidden = pl.pallas_call(
        functools.partial(kernel, dims),
        out_shape=[
            jax.ShapeDtypeStruct(cg_shape, BF16),
            jax.ShapeDtypeStruct(hid_shape, BF16),
        ],
        in_specs=[vmem] * 7 + [hbm],
        out_specs=[hbm, hbm],
        scratch_shapes=[
            pltpu.VMEM((slots, lanes), BF16),
            pltpu.VMEM((slots, lanes), BF16),
            pltpu.VMEM((lev, slots), BF16),
            pltpu.VMEM((slots, tile_lat), BF16),
            pltpu.VMEM(cg_shape, BF16),
            pltpu.VMEM(hid_shape, F32),
            pltpu.VMEM(hid_shape, BF16),
            pltpu.VMEM((layers, 2, (quads + 2) * width, 2 * tile_lat), BF16),
            pltpu.VMEM((2, width, tile_lon, tile_lat), BF16),
            pltpu.VMEM((layers, width * tile_lon, tile_lat), F32),
            pltpu.VMEM((layers, width, 3 * width), BF16),
            pltpu.VMEM((width, lev), BF16),
            pltpu.VMEM((lanes, width), F32),
            pltpu.VMEM((lev * kinds_n, channels), F32),
            pltpu.VMEM((lev, kinds_n * channels), BF16),
            dma((devices,)),
            dma((devices,)),
            dma((layers, 2, 2)),
            dma((layers, 2, 2)),
            dma((2,)),
            dma((4,)),
        ],
        compiler_params=pltpu.CompilerParams(
            collective_id=0, has_side_effects=True, vmem_limit_bytes=60 * 1024 * 1024
        ),
    )(
        observation_residual, obs_index, obs_count, obs_weight.reshape(1, channels),
        jnp.transpose(jacobian, (2, 1, 0)), decoder, conv_weight, gates,
    )
    return pl.pallas_call(
        encode_kernel,
        out_shape=jax.ShapeDtypeStruct((levels, tile_lon, tile_lat), F32),
        grid=(quads // 2,),
        in_specs=[
            pl.BlockSpec((2, 2, lev, 2 * tile_lat), lambda p: (0, p, 0, 0)),
            pl.BlockSpec((2, 2, width, 2 * tile_lat), lambda p: (0, p, 0, 0)),
            pl.BlockSpec((levels, width), lambda p: (0, 0)),
        ],
        out_specs=pl.BlockSpec((levels, 8, tile_lat), lambda p: (0, p, 0)),
        compiler_params=pltpu.CompilerParams(vmem_limit_bytes=32 * 1024 * 1024),
    )(column_grad, hidden, jnp.transpose(encoder))


def solution(mesh):
    return jax.shard_map(
        per_device,
        mesh=mesh,
        in_specs=(
            P(None, ("lat", "lon")),
            P(None, ("lat", "lon")),
            P(None, ("lat", "lon")),
            P(),
            P(),
            P(),
            P(),
            P(None, None, "lon", "lat"),
            P(),
        ),
        out_specs=P(None, "lon", "lat"),
        check_vma=False,
    )
```

```python
import functools

import jax
import jax.numpy as jnp
from jax import lax
from jax.experimental import pallas as pl
from jax.experimental.pallas import tpu as pltpu
from jax.sharding import PartitionSpec as P

MESH = pl.DeviceIdType.MESH
F32 = jnp.float32
BF16 = jnp.bfloat16


def up(value, unit):
    return (value + unit - 1) // unit * unit


def odd(rows):
    return rows // 2 * 2 + 1


def kernel(
    dims,
    resid, index, counts, weight, jac, dec, conv, gates, cg_out, hid_out,
    sent, got, incr, place, cg, hid, last, field, stage, gate, taps, dec_t, tall, blocks, jac_l,
    a2a_send, a2a_recv, halo_send, halo_recv, gate_sem, out_sem,
):
    lat_n, lon_n, slot, kinds_n, levels, layers, width, tile_lon, tile_lat = dims
    devices = lat_n * lon_n
    lev = incr.shape[0]
    quads = tile_lon // 4
    pitch = odd(tile_lon)
    my_lat, my_lon = lax.axis_index("lat"), lax.axis_index("lon")
    me = my_lat * lon_n + my_lon
    right, left = lax.rem(my_lon + 1, lon_n), lax.rem(my_lon + lon_n - 1, lon_n)

    def gate_copy(layer):
        return pltpu.make_async_copy(gates.at[layer], stage.at[layer % 2], gate_sem.at[layer % 2])

    order = list(reversed(range(layers)))
    for layer in order[:2]:
        gate_copy(layer).start()

    barrier = pltpu.get_barrier_semaphore()

    @pl.loop(1, devices)
    def _(off):
        d = lax.rem(me + off, devices)
        pl.semaphore_signal(
            barrier, inc=1, device_id=(d // lon_n, lax.rem(d, lon_n)), device_id_type=MESH
        )

    channels = resid.shape[0]
    blocks[...] = jnp.zeros_like(blocks)
    blocks[0 : levels * kinds_n, :] = jac[...].astype(F32).reshape(levels * kinds_n, -1)
    for k in range(kinds_n):
        jac_l[:, k * channels : (k + 1) * channels] = blocks[pl.ds(k, lev, stride=kinds_n), :].astype(BF16)
    weight_lanes = jnp.transpose(jnp.broadcast_to(weight[...], (128, weight.shape[1])))
    counts8 = jnp.broadcast_to(counts[...].astype(F32), (8, devices)).astype(BF16)
    mine = pl.ds(pl.multiple_of(me * slot, slot), slot)

    def slots_to(d):
        return pltpu.make_async_remote_copy(
            src_ref=sent.at[pl.ds(pl.multiple_of(d * slot, slot), slot)],
            dst_ref=got.at[mine],
            send_sem=a2a_send.at[d],
            recv_sem=a2a_recv.at[me],
            device_id=(d // lon_n, lax.rem(d, lon_n)),
            device_id_type=MESH,
        )

    def slots_from(s):
        return pltpu.make_async_remote_copy(
            src_ref=sent.at[mine],
            dst_ref=got.at[pl.ds(pl.multiple_of(s * slot, slot), slot)],
            send_sem=a2a_send.at[s],
            recv_sem=a2a_recv.at[s],
            device_id=(s // lon_n, lax.rem(s, lon_n)),
            device_id_type=MESH,
        )

    pl.semaphore_wait(barrier, devices - 1)

    chunks = devices * slot // 128
    per_chunk = 128 // slot

    @pl.loop(0, chunks)
    def _(turn):
        chunk = lax.rem(turn + me // per_chunk + 1, chunks)
        lanes = pl.ds(pl.multiple_of(chunk * 128, 128), 128)
        pair = (lax.broadcasted_iota(jnp.int32, (devices, 128), 1) + chunk * 128) // slot
        owner = lax.broadcasted_iota(jnp.int32, (devices, 128), 0)
        spread = jnp.where(pair == owner, 1.0, 0.0).astype(BF16)
        limit = jnp.dot(counts8, spread, preferred_element_type=F32)[0:1]
        nth = lax.broadcasted_iota(jnp.int32, (1, 128), 1) % slot
        used = nth.astype(F32) < limit
        weighted = jnp.where(used, weight_lanes * resid[:, lanes].astype(F32), 0.0)
        kinds = index[1:2, lanes]
        cells = index[0:1, lanes]
        stack = jnp.concatenate(
            [jnp.where(kinds == k, weighted, 0.0).astype(BF16) for k in range(kinds_n)], axis=0
        )
        value = jnp.dot(jac_l[...], stack, preferred_element_type=F32)
        row = lax.broadcasted_iota(jnp.int32, (lev, 128), 0)
        lon = (cells // tile_lat).astype(F32)
        lat = (cells % tile_lat).astype(F32)
        value = jnp.where(row == levels, lon, jnp.where(row == levels + 1, lat, value))
        pad = jnp.zeros((sent.shape[1] - lev, 128), F32)
        sent[lanes, :] = jnp.transpose(jnp.concatenate([value, pad], axis=0)).astype(BF16)

        @pl.loop(0, per_chunk)
        def _(nth):
            d = chunk * per_chunk + lax.rem(nth + me, per_chunk)

            @pl.when(d != me)
            def _():
                slots_to(d).start()

    got[mine, :] = sent[mine, :]

    for layer in range(layers):
        for tap in range(3):
            taps[layer, :, (2 - tap) * width : (3 - tap) * width] = jnp.transpose(
                conv[layer, tap].astype(F32)
            ).astype(BF16)
    tall[...] = jnp.zeros_like(tall)
    tall[0:levels, :] = dec[...].astype(F32)
    dec_t[...] = jnp.transpose(tall[...])[:, 0:lev].astype(BF16)

    for at, layer in enumerate(order):
        gate_copy(layer).wait()

        @pl.loop(0, width // 4)
        def _(block):
            for part in range(4):
                c = block * 4 + part
                gate[layer, pl.ds(c * pitch, tile_lon), :] = stage[layer % 2, c].astype(F32)

        if at + 2 < layers:
            gate_copy(order[at + 2]).start()

    @pl.loop(1, devices)
    def _(off):
        s = lax.rem(me + devices - off, devices)
        slots_from(s).wait_recv()

    @pl.loop(0, devices * slot // 128)
    def _(chunk):
        lanes = pl.ds(pl.multiple_of(chunk * 128, 128), 128)
        block = got[lanes, :].astype(F32)
        incr[:, lanes] = jnp.transpose(block)[0:lev].astype(BF16)
        lane = lax.broadcasted_iota(jnp.int32, (128, tile_lat), 1).astype(F32)
        at_lat = block[:, levels + 1 : levels + 2] == lane
        place[lanes, :] = jnp.where(at_lat, block[:, levels : levels + 1], -1.0).astype(BF16)

    def rows_of(q):
        return pl.ds(pl.multiple_of(q * width, width), width)

    def halos(layer, rp):
        to_right = pltpu.make_async_remote_copy(
            src_ref=field.at[layer, rp, rows_of(quads)],
            dst_ref=field.at[layer, rp, rows_of(0)],
            send_sem=halo_send.at[layer, rp, 0],
            recv_sem=halo_recv.at[layer, rp, 0],
            device_id=(my_lat, right),
            device_id_type=MESH,
        )
        to_left = pltpu.make_async_remote_copy(
            src_ref=field.at[layer, rp, rows_of(1)],
            dst_ref=field.at[layer, rp, rows_of(quads + 1)],
            send_sem=halo_send.at[layer, rp, 1],
            recv_sem=halo_recv.at[layer, rp, 1],
            device_id=(my_lat, left),
            device_id_type=MESH,
        )
        return to_right, to_left

    def scatter(rp, q):
        lon = 4 * (q - 1) + 2 * rp
        hot = []
        for r in range(2):
            value = jnp.full((1, tile_lat), lon + r, jnp.int32).astype(F32).astype(BF16)
            hot.append(jnp.where(place[...] == value, 1.0, 0.0).astype(BF16))
        total = jnp.dot(incr[...], jnp.concatenate(hot, axis=1), preferred_element_type=F32)
        narrow = total.astype(BF16)
        cg[rp, q - 1] = narrow
        hidden = jnp.dot(dec_t[...], narrow, preferred_element_type=F32)
        hid[rp, q - 1] = hidden
        field[layers - 1, rp, rows_of(q), :] = hidden.astype(BF16)

    def conv_at(layer, rp, q):
        window = field[layer, rp, pl.ds(pl.multiple_of((q - 1) * width, width), 3 * width), :]
        back = jnp.dot(taps[layer], window, preferred_element_type=F32)
        lon = 4 * (q - 1) + 2 * rp
        parts = []
        for r in range(2):
            lats = slice(r * tile_lat, (r + 1) * tile_lat)
            factor = gate[layer, pl.ds(lon + r, width, stride=pitch), :]
            parts.append(hid[rp, q - 1, :, lats] + factor * back[:, lats])
        return jnp.concatenate(parts, axis=1)

    def step(layer, rp, q):
        hidden = conv_at(layer, rp, q)
        hid[rp, q - 1] = hidden
        field[layer - 1, rp, rows_of(q), :] = hidden.astype(BF16)

    def edges_then_inside(visit, layer):
        for rp in range(2):
            visit(rp, 1)
            visit(rp, quads)
            for copy in halos(layer, rp):
                copy.start()

        @pl.loop(2, quads)
        def _(q):
            for rp in range(2):
                visit(rp, q)

    edges_then_inside(scatter, layers - 1)
    cg_copy = pltpu.make_async_copy(cg, cg_out, out_sem.at[0])
    cg_copy.start()
    for layer in reversed(range(1, layers)):
        for rp in range(2):
            for copy in halos(layer, rp):
                copy.wait_recv()
        edges_then_inside(functools.partial(step, layer), layer - 1)

    def finish(q):
        for rp in range(2):
            last[rp, q - 1] = conv_at(0, rp, q).astype(BF16)

    def hid_copy(start, count, sem):
        part = pl.ds(start, count)
        return pltpu.make_async_copy(last.at[:, part], hid_out.at[:, part], out_sem.at[sem])

    pl.loop(2, quads)(finish)
    hid_copy(1, quads - 2, 1).start()
    for rp in range(2):
        for copy in halos(0, rp):
            copy.wait_recv()
    finish(1)
    hid_copy(0, 1, 2).start()
    finish(quads)
    hid_copy(quads - 1, 1, 3).start()

    @pl.loop(1, devices)
    def _(off):
        slots_to(lax.rem(me + off, devices)).wait_send()

    for layer in range(layers):
        for rp in range(2):
            for copy in halos(layer, rp):
                copy.wait_send()

    cg_copy.wait()
    hid_copy(1, quads - 2, 1).wait()
    hid_copy(0, 1, 2).wait()
    hid_copy(quads - 1, 1, 3).wait()


def encode_kernel(cg, hid, enc, out, slabs):
    levels, lons, tile_lat = out.shape
    pitch = odd(levels)
    for half in range(2):
        for rp in range(2):
            state = cg[rp, half, 0:levels].astype(F32) + jnp.dot(
                enc[...], hid[rp, half], preferred_element_type=F32
            )
            for r in range(2):
                lon = half * 4 + rp * 2 + r
                slabs[lon * pitch : lon * pitch + levels, :] = state[
                    :, r * tile_lat : (r + 1) * tile_lat
                ]
    for level in range(levels):
        out[level] = slabs[pl.ds(level, lons, stride=pitch), :]


def per_device(
    observation_residual, obs_index, obs_count, obs_weight, jacobian, decoder, conv_weight, gates, encoder
):
    lat_n, lon_n = lax.axis_size("lat"), lax.axis_size("lon")
    devices = lat_n * lon_n
    channels, slots = observation_residual.shape
    slot = slots // devices
    kinds_n, levels = jacobian.shape[1:]
    layers, width, tile_lon, tile_lat = gates.shape
    lev = up(levels + 2, 16)
    lanes = up(levels + 2, 128)
    quads = tile_lon // 4

    dims = (lat_n, lon_n, slot, kinds_n, levels, layers, width, tile_lon, tile_lat)
    vmem = pl.BlockSpec(memory_space=pltpu.VMEM)
    hbm = pl.BlockSpec(memory_space=pl.ANY)
    dma = pltpu.SemaphoreType.DMA
    cg_shape = (2, quads, lev, 2 * tile_lat)
    hid_shape = (2, quads, width, 2 * tile_lat)
    column_grad, hidden = pl.pallas_call(
        functools.partial(kernel, dims),
        out_shape=[
            jax.ShapeDtypeStruct(cg_shape, BF16),
            jax.ShapeDtypeStruct(hid_shape, BF16),
        ],
        in_specs=[vmem] * 7 + [hbm],
        out_specs=[hbm, hbm],
        scratch_shapes=[
            pltpu.VMEM((slots, lanes), BF16),
            pltpu.VMEM((slots, lanes), BF16),
            pltpu.VMEM((lev, slots), BF16),
            pltpu.VMEM((slots, tile_lat), BF16),
            pltpu.VMEM(cg_shape, BF16),
            pltpu.VMEM(hid_shape, F32),
            pltpu.VMEM(hid_shape, BF16),
            pltpu.VMEM((layers, 2, (quads + 2) * width, 2 * tile_lat), BF16),
            pltpu.VMEM((2, width, tile_lon, tile_lat), BF16),
            pltpu.VMEM((layers, up(width * odd(tile_lon), 8), tile_lat), F32),
            pltpu.VMEM((layers, width, 3 * width), BF16),
            pltpu.VMEM((width, lev), BF16),
            pltpu.VMEM((lanes, width), F32),
            pltpu.VMEM((lev * kinds_n, channels), F32),
            pltpu.VMEM((lev, kinds_n * channels), BF16),
            dma((devices,)),
            dma((devices,)),
            dma((layers, 2, 2)),
            dma((layers, 2, 2)),
            dma((2,)),
            dma((4,)),
        ],
        compiler_params=pltpu.CompilerParams(
            collective_id=0, has_side_effects=True, vmem_limit_bytes=60 * 1024 * 1024
        ),
    )(
        observation_residual, obs_index, obs_count, obs_weight.reshape(1, channels),
        jnp.transpose(jacobian, (2, 1, 0)), decoder, conv_weight, gates,
    )
    return pl.pallas_call(
        encode_kernel,
        out_shape=jax.ShapeDtypeStruct((levels, tile_lon, tile_lat), F32),
        grid=(quads // 2,),
        in_specs=[
            pl.BlockSpec((2, 2, lev, 2 * tile_lat), lambda p: (0, p, 0, 0)),
            pl.BlockSpec((2, 2, width, 2 * tile_lat), lambda p: (0, p, 0, 0)),
            pl.BlockSpec((levels, width), lambda p: (0, 0)),
        ],
        out_specs=pl.BlockSpec((levels, 8, tile_lat), lambda p: (0, p, 0)),
        scratch_shapes=[pltpu.VMEM((up(8 * odd(levels), 8), tile_lat), F32)],
        compiler_params=pltpu.CompilerParams(vmem_limit_bytes=60 * 1024 * 1024),
    )(column_grad, hidden, jnp.transpose(encoder))


def solution(mesh):
    return jax.shard_map(
        per_device,
        mesh=mesh,
        in_specs=(
            P(None, ("lat", "lon")),
            P(None, ("lat", "lon")),
            P(None, ("lat", "lon")),
            P(),
            P(),
            P(),
            P(),
            P(None, None, "lon", "lat"),
            P(),
        ),
        out_specs=P(None, "lon", "lat"),
        check_vma=False,
    )
```

```python
import functools

import jax
import jax.numpy as jnp
from jax import lax
from jax.experimental import pallas as pl
from jax.experimental.pallas import tpu as pltpu
from jax.sharding import PartitionSpec as P

MESH = pl.DeviceIdType.MESH
F32 = jnp.float32
BF16 = jnp.bfloat16


def up(value, unit):
    return (value + unit - 1) // unit * unit


def odd(rows):
    return rows // 2 * 2 + 1


def kernel(
    dims,
    resid, index, counts, weight, jac, dec, conv, gates, cg_out, hid_out,
    sent, got, incr, place, cg, hid, last, field, stage, gate, taps, dec_t, tall, blocks, jac_l,
    a2a_send, a2a_recv, halo_send, halo_recv, gate_sem, out_sem,
):
    lat_n, lon_n, slot, kinds_n, levels, layers, width, tile_lon, tile_lat = dims
    devices = lat_n * lon_n
    lev = incr.shape[0]
    quads = tile_lon // 4
    pitch = odd(tile_lon)
    my_lat, my_lon = lax.axis_index("lat"), lax.axis_index("lon")
    me = my_lat * lon_n + my_lon
    right, left = lax.rem(my_lon + 1, lon_n), lax.rem(my_lon + lon_n - 1, lon_n)

    def gate_copy(layer):
        return pltpu.make_async_copy(gates.at[layer], stage.at[layer % 2], gate_sem.at[layer % 2])

    order = list(reversed(range(layers)))
    for layer in order[:2]:
        gate_copy(layer).start()

    barrier = pltpu.get_barrier_semaphore()

    @pl.loop(1, devices)
    def _(off):
        d = lax.rem(me + off, devices)
        pl.semaphore_signal(
            barrier, inc=1, device_id=(d // lon_n, lax.rem(d, lon_n)), device_id_type=MESH
        )

    channels = resid.shape[0]
    blocks[...] = jnp.zeros_like(blocks)
    blocks[0 : levels * kinds_n, :] = jac[...].astype(F32).reshape(levels * kinds_n, -1)
    for k in range(kinds_n):
        jac_l[:, k * channels : (k + 1) * channels] = blocks[pl.ds(k, lev, stride=kinds_n), :].astype(BF16)
    weight_lanes = jnp.transpose(jnp.broadcast_to(weight[...], (128, weight.shape[1])))
    counts8 = jnp.broadcast_to(counts[...].astype(F32), (8, devices)).astype(BF16)
    mine = pl.ds(pl.multiple_of(me * slot, slot), slot)

    def slots_to(d):
        return pltpu.make_async_remote_copy(
            src_ref=sent.at[pl.ds(pl.multiple_of(d * slot, slot), slot)],
            dst_ref=got.at[mine],
            send_sem=a2a_send.at[d],
            recv_sem=a2a_recv.at[me],
            device_id=(d // lon_n, lax.rem(d, lon_n)),
            device_id_type=MESH,
        )

    def slots_from(s):
        return pltpu.make_async_remote_copy(
            src_ref=sent.at[mine],
            dst_ref=got.at[pl.ds(pl.multiple_of(s * slot, slot), slot)],
            send_sem=a2a_send.at[s],
            recv_sem=a2a_recv.at[s],
            device_id=(s // lon_n, lax.rem(s, lon_n)),
            device_id_type=MESH,
        )

    pl.semaphore_wait(barrier, devices - 1)

    chunks = devices * slot // 128
    per_chunk = 128 // slot

    @pl.loop(0, chunks)
    def _(turn):
        chunk = lax.rem(turn + me // per_chunk + 1, chunks)
        lanes = pl.ds(pl.multiple_of(chunk * 128, 128), 128)
        pair = (lax.broadcasted_iota(jnp.int32, (devices, 128), 1) + chunk * 128) // slot
        owner = lax.broadcasted_iota(jnp.int32, (devices, 128), 0)
        spread = jnp.where(pair == owner, 1.0, 0.0).astype(BF16)
        limit = jnp.dot(counts8, spread, preferred_element_type=F32)[0:1]
        nth = lax.broadcasted_iota(jnp.int32, (1, 128), 1) % slot
        used = nth.astype(F32) < limit
        weighted = jnp.where(used, weight_lanes * resid[:, lanes].astype(F32), 0.0)
        kinds = index[1:2, lanes]
        cells = index[0:1, lanes]
        stack = jnp.concatenate(
            [jnp.where(kinds == k, weighted, 0.0).astype(BF16) for k in range(kinds_n)], axis=0
        )
        value = jnp.dot(jac_l[...], stack, preferred_element_type=F32)
        row = lax.broadcasted_iota(jnp.int32, (lev, 128), 0)
        lon = (cells // tile_lat).astype(F32)
        lat = (cells % tile_lat).astype(F32)
        value = jnp.where(row == levels, lon, jnp.where(row == levels + 1, lat, value))
        pad = jnp.zeros((sent.shape[1] - lev, 128), F32)
        sent[lanes, :] = jnp.transpose(jnp.concatenate([value, pad], axis=0)).astype(BF16)

        @pl.loop(0, per_chunk)
        def _(nth):
            d = chunk * per_chunk + lax.rem(nth + me, per_chunk)

            @pl.when(d != me)
            def _():
                slots_to(d).start()

    got[mine, :] = sent[mine, :]

    for layer in range(layers):
        for tap in range(3):
            taps[layer, :, (2 - tap) * width : (3 - tap) * width] = jnp.transpose(
                conv[layer, tap].astype(F32)
            ).astype(BF16)
    tall[...] = jnp.zeros_like(tall)
    tall[0:levels, :] = dec[...].astype(F32)
    dec_t[...] = jnp.transpose(tall[...])[:, 0:lev].astype(BF16)

    def open_gate(layer):
        gate_copy(layer).wait()

        @pl.loop(0, width // 4)
        def _(block):
            for part in range(4):
                c = block * 4 + part
                gate[layer, pl.ds(c * pitch, tile_lon), :] = stage[layer % 2, c].astype(F32)

        if layer >= 2:
            gate_copy(layer - 2).start()

    @pl.loop(1, devices)
    def _(off):
        s = lax.rem(me + devices - off, devices)
        slots_from(s).wait_recv()

    @pl.loop(0, devices * slot // 128)
    def _(chunk):
        lanes = pl.ds(pl.multiple_of(chunk * 128, 128), 128)
        block = got[lanes, :].astype(F32)
        incr[:, lanes] = jnp.transpose(block)[0:lev].astype(BF16)
        lane = lax.broadcasted_iota(jnp.int32, (128, tile_lat), 1).astype(F32)
        at_lat = block[:, levels + 1 : levels + 2] == lane
        place[lanes, :] = jnp.where(at_lat, block[:, levels : levels + 1], -1.0).astype(BF16)

    def rows_of(q):
        return pl.ds(pl.multiple_of(q * width, width), width)

    def halos(layer, rp):
        to_right = pltpu.make_async_remote_copy(
            src_ref=field.at[layer, rp, rows_of(quads)],
            dst_ref=field.at[layer, rp, rows_of(0)],
            send_sem=halo_send.at[layer, rp, 0],
            recv_sem=halo_recv.at[layer, rp, 0],
            device_id=(my_lat, right),
            device_id_type=MESH,
        )
        to_left = pltpu.make_async_remote_copy(
            src_ref=field.at[layer, rp, rows_of(1)],
            dst_ref=field.at[layer, rp, rows_of(quads + 1)],
            send_sem=halo_send.at[layer, rp, 1],
            recv_sem=halo_recv.at[layer, rp, 1],
            device_id=(my_lat, left),
            device_id_type=MESH,
        )
        return to_right, to_left

    def scatter(rp, q):
        lon = 4 * (q - 1) + 2 * rp
        hot = []
        for r in range(2):
            value = jnp.full((1, tile_lat), lon + r, jnp.int32).astype(F32).astype(BF16)
            hot.append(jnp.where(place[...] == value, 1.0, 0.0).astype(BF16))
        total = jnp.dot(incr[...], jnp.concatenate(hot, axis=1), preferred_element_type=F32)
        narrow = total.astype(BF16)
        cg[rp, q - 1] = narrow
        hidden = jnp.dot(dec_t[...], narrow, preferred_element_type=F32)
        hid[rp, q - 1] = hidden
        field[layers - 1, rp, rows_of(q), :] = hidden.astype(BF16)

    def conv_at(layer, rp, q):
        window = field[layer, rp, pl.ds(pl.multiple_of((q - 1) * width, width), 3 * width), :]
        back = jnp.dot(taps[layer], window, preferred_element_type=F32)
        lon = 4 * (q - 1) + 2 * rp
        parts = []
        for r in range(2):
            lats = slice(r * tile_lat, (r + 1) * tile_lat)
            factor = gate[layer, pl.ds(lon + r, width, stride=pitch), :]
            parts.append(hid[rp, q - 1, :, lats] + factor * back[:, lats])
        return jnp.concatenate(parts, axis=1)

    def step(layer, rp, q):
        hidden = conv_at(layer, rp, q)
        hid[rp, q - 1] = hidden
        field[layer - 1, rp, rows_of(q), :] = hidden.astype(BF16)

    def edges_then_inside(visit, layer):
        for rp in range(2):
            visit(rp, 1)
            visit(rp, quads)
            for copy in halos(layer, rp):
                copy.start()

        @pl.loop(2, quads)
        def _(q):
            for rp in range(2):
                visit(rp, q)

    edges_then_inside(scatter, layers - 1)
    cg_copy = pltpu.make_async_copy(cg, cg_out, out_sem.at[0])
    cg_copy.start()
    for layer in reversed(range(1, layers)):
        open_gate(layer)
        for rp in range(2):
            for copy in halos(layer, rp):
                copy.wait_recv()
        edges_then_inside(functools.partial(step, layer), layer - 1)

    def finish(q):
        for rp in range(2):
            last[rp, q - 1] = conv_at(0, rp, q).astype(BF16)

    def hid_copy(start, count, sem):
        part = pl.ds(start, count)
        return pltpu.make_async_copy(last.at[:, part], hid_out.at[:, part], out_sem.at[sem])

    open_gate(0)
    pl.loop(2, quads)(finish)
    hid_copy(1, quads - 2, 1).start()
    for rp in range(2):
        for copy in halos(0, rp):
            copy.wait_recv()
    finish(1)
    hid_copy(0, 1, 2).start()
    finish(quads)
    hid_copy(quads - 1, 1, 3).start()

    @pl.loop(1, devices)
    def _(off):
        slots_to(lax.rem(me + off, devices)).wait_send()

    for layer in range(layers):
        for rp in range(2):
            for copy in halos(layer, rp):
                copy.wait_send()

    cg_copy.wait()
    hid_copy(1, quads - 2, 1).wait()
    hid_copy(0, 1, 2).wait()
    hid_copy(quads - 1, 1, 3).wait()


def encode_kernel(cg_in, hid_in, enc, out, cg, hid, slabs, done, in_sem, out_sem):
    pairs, levels, lons, tile_lat = done.shape
    pitch = odd(levels)

    def reads(pair):
        part = pl.ds(2 * pair, 2)
        return (
            pltpu.make_async_copy(cg_in.at[:, part], cg.at[:, part], in_sem.at[pair, 0]),
            pltpu.make_async_copy(hid_in.at[:, part], hid.at[:, part], in_sem.at[pair, 1]),
        )

    def write(pair):
        part = pl.ds(pl.multiple_of(lons * pair, lons), lons)
        return pltpu.make_async_copy(done.at[pair], out.at[:, part, :], out_sem.at[pair])

    @pl.loop(0, pairs)
    def _(pair):
        for copy in reads(pair):
            copy.start()

    @pl.loop(0, pairs)
    def _(pair):
        for copy in reads(pair):
            copy.wait()
        for half in range(2):
            for rp in range(2):
                q = 2 * pair + half
                state = cg[rp, q, 0:levels].astype(F32) + jnp.dot(
                    enc[...], hid[rp, q], preferred_element_type=F32
                )
                for r in range(2):
                    lon = half * 4 + rp * 2 + r
                    slabs[lon * pitch : lon * pitch + levels, :] = state[
                        :, r * tile_lat : (r + 1) * tile_lat
                    ]
        for level in range(levels):
            done[pair, level] = slabs[pl.ds(level, lons, stride=pitch), :]
        write(pair).start()

    @pl.loop(0, pairs)
    def _(pair):
        write(pair).wait()


def per_device(
    observation_residual, obs_index, obs_count, obs_weight, jacobian, decoder, conv_weight, gates, encoder
):
    lat_n, lon_n = lax.axis_size("lat"), lax.axis_size("lon")
    devices = lat_n * lon_n
    channels, slots = observation_residual.shape
    slot = slots // devices
    kinds_n, levels = jacobian.shape[1:]
    layers, width, tile_lon, tile_lat = gates.shape
    lev = up(levels + 2, 16)
    lanes = up(levels + 2, 128)
    quads = tile_lon // 4

    dims = (lat_n, lon_n, slot, kinds_n, levels, layers, width, tile_lon, tile_lat)
    vmem = pl.BlockSpec(memory_space=pltpu.VMEM)
    hbm = pl.BlockSpec(memory_space=pl.ANY)
    dma = pltpu.SemaphoreType.DMA
    cg_shape = (2, quads, lev, 2 * tile_lat)
    hid_shape = (2, quads, width, 2 * tile_lat)
    column_grad, hidden = pl.pallas_call(
        functools.partial(kernel, dims),
        out_shape=[
            jax.ShapeDtypeStruct(cg_shape, BF16),
            jax.ShapeDtypeStruct(hid_shape, BF16),
        ],
        in_specs=[vmem] * 7 + [hbm],
        out_specs=[hbm, hbm],
        scratch_shapes=[
            pltpu.VMEM((slots, lanes), BF16),
            pltpu.VMEM((slots, lanes), BF16),
            pltpu.VMEM((lev, slots), BF16),
            pltpu.VMEM((slots, tile_lat), BF16),
            pltpu.VMEM(cg_shape, BF16),
            pltpu.VMEM(hid_shape, F32),
            pltpu.VMEM(hid_shape, BF16),
            pltpu.VMEM((layers, 2, (quads + 2) * width, 2 * tile_lat), BF16),
            pltpu.VMEM((2, width, tile_lon, tile_lat), BF16),
            pltpu.VMEM((layers, up(width * odd(tile_lon), 8), tile_lat), F32),
            pltpu.VMEM((layers, width, 3 * width), BF16),
            pltpu.VMEM((width, lev), BF16),
            pltpu.VMEM((lanes, width), F32),
            pltpu.VMEM((lev * kinds_n, channels), F32),
            pltpu.VMEM((lev, kinds_n * channels), BF16),
            dma((devices,)),
            dma((devices,)),
            dma((layers, 2, 2)),
            dma((layers, 2, 2)),
            dma((2,)),
            dma((4,)),
        ],
        compiler_params=pltpu.CompilerParams(
            collective_id=0, has_side_effects=True, vmem_limit_bytes=60 * 1024 * 1024
        ),
    )(
        observation_residual, obs_index, obs_count, obs_weight.reshape(1, channels),
        jnp.transpose(jacobian, (2, 1, 0)), decoder, conv_weight, gates,
    )
    return pl.pallas_call(
        encode_kernel,
        out_shape=jax.ShapeDtypeStruct((levels, tile_lon, tile_lat), F32),
        in_specs=[hbm, hbm, vmem],
        out_specs=hbm,
        scratch_shapes=[
            pltpu.VMEM(cg_shape, BF16),
            pltpu.VMEM(hid_shape, BF16),
            pltpu.VMEM((up(8 * odd(levels), 8), tile_lat), F32),
            pltpu.VMEM((quads // 2, levels, 8, tile_lat), F32),
            dma((quads // 2, 2)),
            dma((quads // 2,)),
        ],
        compiler_params=pltpu.CompilerParams(vmem_limit_bytes=60 * 1024 * 1024),
    )(column_grad, hidden, jnp.transpose(encoder))


def solution(mesh):
    return jax.shard_map(
        per_device,
        mesh=mesh,
        in_specs=(
            P(None, ("lat", "lon")),
            P(None, ("lat", "lon")),
            P(None, ("lat", "lon")),
            P(),
            P(),
            P(),
            P(),
            P(None, None, "lon", "lat"),
            P(),
        ),
        out_specs=P(None, "lon", "lat"),
        check_vma=False,
    )
```

```python
import functools

import jax
import jax.numpy as jnp
from jax import lax
from jax.experimental import pallas as pl
from jax.experimental.pallas import tpu as pltpu
from jax.sharding import PartitionSpec as P

MESH = pl.DeviceIdType.MESH
F32 = jnp.float32
BF16 = jnp.bfloat16


def up(value, unit):
    return (value + unit - 1) // unit * unit


def odd(rows):
    return rows // 2 * 2 + 1


def kernel(
    dims,
    resid, index, counts, weight, jac, dec, conv, gates, cg_out, hid_out,
    sent, got, incr, place, cg, hid, last, field, stage, gate, taps, dec_t, tall, blocks, jac_l,
    a2a_send, a2a_recv, halo_send, halo_recv, gate_sem, out_sem,
):
    lat_n, lon_n, slot, kinds_n, levels, layers, width, tile_lon, tile_lat = dims
    devices = lat_n * lon_n
    lev = incr.shape[0]
    quads = tile_lon // 4
    pitch = odd(tile_lon)
    my_lat, my_lon = lax.axis_index("lat"), lax.axis_index("lon")
    me = my_lat * lon_n + my_lon
    right, left = lax.rem(my_lon + 1, lon_n), lax.rem(my_lon + lon_n - 1, lon_n)

    def gate_copy(layer):
        return pltpu.make_async_copy(gates.at[layer], stage.at[layer % 2], gate_sem.at[layer % 2])

    order = list(reversed(range(layers)))
    for layer in order[:2]:
        gate_copy(layer).start()

    barrier = pltpu.get_barrier_semaphore()

    @pl.loop(1, devices)
    def _(off):
        d = lax.rem(me + off, devices)
        pl.semaphore_signal(
            barrier, inc=1, device_id=(d // lon_n, lax.rem(d, lon_n)), device_id_type=MESH
        )

    channels = resid.shape[0]
    blocks[...] = jnp.zeros_like(blocks)
    blocks[0 : levels * kinds_n, :] = jac[...].astype(F32).reshape(levels * kinds_n, -1)
    for k in range(kinds_n):
        jac_l[:, k * channels : (k + 1) * channels] = blocks[pl.ds(k, lev, stride=kinds_n), :].astype(BF16)
    weight_lanes = jnp.transpose(jnp.broadcast_to(weight[...], (128, weight.shape[1])))
    counts8 = jnp.broadcast_to(counts[...].astype(F32), (8, devices)).astype(BF16)
    mine = pl.ds(pl.multiple_of(me * slot, slot), slot)

    def slots_to(d):
        return pltpu.make_async_remote_copy(
            src_ref=sent.at[pl.ds(pl.multiple_of(d * slot, slot), slot)],
            dst_ref=got.at[mine],
            send_sem=a2a_send.at[d],
            recv_sem=a2a_recv.at[me],
            device_id=(d // lon_n, lax.rem(d, lon_n)),
            device_id_type=MESH,
        )

    def slots_from(s):
        return pltpu.make_async_remote_copy(
            src_ref=sent.at[mine],
            dst_ref=got.at[pl.ds(pl.multiple_of(s * slot, slot), slot)],
            send_sem=a2a_send.at[s],
            recv_sem=a2a_recv.at[s],
            device_id=(s // lon_n, lax.rem(s, lon_n)),
            device_id_type=MESH,
        )

    pl.semaphore_wait(barrier, devices - 1)

    chunks = devices * slot // 128
    per_chunk = 128 // slot

    @pl.loop(0, chunks)
    def _(turn):
        chunk = lax.rem(turn + me // per_chunk + 1, chunks)
        lanes = pl.ds(pl.multiple_of(chunk * 128, 128), 128)
        pair = (lax.broadcasted_iota(jnp.int32, (devices, 128), 1) + chunk * 128) // slot
        owner = lax.broadcasted_iota(jnp.int32, (devices, 128), 0)
        spread = jnp.where(pair == owner, 1.0, 0.0).astype(BF16)
        limit = jnp.dot(counts8, spread, preferred_element_type=F32)[0:1]
        nth = lax.broadcasted_iota(jnp.int32, (1, 128), 1) % slot
        used = nth.astype(F32) < limit
        weighted = jnp.where(used, weight_lanes * resid[:, lanes].astype(F32), 0.0)
        kinds = index[1:2, lanes]
        cells = index[0:1, lanes]
        stack = jnp.concatenate(
            [jnp.where(kinds == k, weighted, 0.0).astype(BF16) for k in range(kinds_n)], axis=0
        )
        value = jnp.dot(jac_l[...], stack, preferred_element_type=F32)
        row = lax.broadcasted_iota(jnp.int32, (lev, 128), 0)
        lon = (cells // tile_lat).astype(F32)
        lat = (cells % tile_lat).astype(F32)
        value = jnp.where(row == levels, lon, jnp.where(row == levels + 1, lat, value))
        pad = jnp.zeros((sent.shape[1] - lev, 128), F32)
        sent[lanes, :] = jnp.transpose(jnp.concatenate([value, pad], axis=0)).astype(BF16)

        @pl.loop(0, per_chunk)
        def _(nth):
            d = chunk * per_chunk + lax.rem(nth + me, per_chunk)

            @pl.when(d != me)
            def _():
                slots_to(d).start()

    got[mine, :] = sent[mine, :]

    for layer in range(layers):
        for tap in range(3):
            taps[layer, :, (2 - tap) * width : (3 - tap) * width] = jnp.transpose(
                conv[layer, tap].astype(F32)
            ).astype(BF16)
    tall[...] = jnp.zeros_like(tall)
    tall[0:levels, :] = dec[...].astype(F32)
    dec_t[...] = jnp.transpose(tall[...])[:, 0:lev].astype(BF16)

    def open_gate(layer):
        gate_copy(layer).wait()

        @pl.loop(0, width // 4)
        def _(block):
            for part in range(4):
                c = block * 4 + part
                gate[layer, pl.ds(c * pitch, tile_lon), :] = stage[layer % 2, c].astype(F32)

        if layer >= 2:
            gate_copy(layer - 2).start()

    for layer in order:
        open_gate(layer)

    @pl.loop(1, devices)
    def _(off):
        s = lax.rem(me + devices - off, devices)
        slots_from(s).wait_recv()

    @pl.loop(0, devices * slot // 128)
    def _(chunk):
        lanes = pl.ds(pl.multiple_of(chunk * 128, 128), 128)
        block = got[lanes, :].astype(F32)
        incr[:, lanes] = jnp.transpose(block)[0:lev].astype(BF16)
        lane = lax.broadcasted_iota(jnp.int32, (128, tile_lat), 1).astype(F32)
        at_lat = block[:, levels + 1 : levels + 2] == lane
        place[lanes, :] = jnp.where(at_lat, block[:, levels : levels + 1], -1.0).astype(BF16)

    def rows_of(q):
        return pl.ds(pl.multiple_of(q * width, width), width)

    def halos(layer, rp):
        to_right = pltpu.make_async_remote_copy(
            src_ref=field.at[layer, rp, rows_of(quads)],
            dst_ref=field.at[layer, rp, rows_of(0)],
            send_sem=halo_send.at[layer, rp, 0],
            recv_sem=halo_recv.at[layer, rp, 0],
            device_id=(my_lat, right),
            device_id_type=MESH,
        )
        to_left = pltpu.make_async_remote_copy(
            src_ref=field.at[layer, rp, rows_of(1)],
            dst_ref=field.at[layer, rp, rows_of(quads + 1)],
            send_sem=halo_send.at[layer, rp, 1],
            recv_sem=halo_recv.at[layer, rp, 1],
            device_id=(my_lat, left),
            device_id_type=MESH,
        )
        return to_right, to_left

    def scatter(rp, q):
        lon = 4 * (q - 1) + 2 * rp
        hot = []
        for r in range(2):
            value = jnp.full((1, tile_lat), lon + r, jnp.int32).astype(F32).astype(BF16)
            hot.append(jnp.where(place[...] == value, 1.0, 0.0).astype(BF16))
        total = jnp.dot(incr[...], jnp.concatenate(hot, axis=1), preferred_element_type=F32)
        narrow = total.astype(BF16)
        cg[rp, q - 1] = narrow
        hidden = jnp.dot(dec_t[...], narrow, preferred_element_type=F32)
        hid[rp, q - 1] = hidden
        field[layers - 1, rp, rows_of(q), :] = hidden.astype(BF16)

    def conv_at(layer, rp, q):
        window = field[layer, rp, pl.ds(pl.multiple_of((q - 1) * width, width), 3 * width), :]
        back = jnp.dot(taps[layer], window, preferred_element_type=F32)
        lon = 4 * (q - 1) + 2 * rp
        parts = []
        for r in range(2):
            lats = slice(r * tile_lat, (r + 1) * tile_lat)
            factor = gate[layer, pl.ds(lon + r, width, stride=pitch), :]
            parts.append(hid[rp, q - 1, :, lats] + factor * back[:, lats])
        return jnp.concatenate(parts, axis=1)

    def step(layer, rp, q):
        hidden = conv_at(layer, rp, q)
        hid[rp, q - 1] = hidden
        field[layer - 1, rp, rows_of(q), :] = hidden.astype(BF16)

    def edges_then_inside(visit, layer):
        for rp in range(2):
            visit(rp, 1)
            visit(rp, quads)
            for copy in halos(layer, rp):
                copy.start()

        @pl.loop(2, quads)
        def _(q):
            for rp in range(2):
                visit(rp, q)

    edges_then_inside(scatter, layers - 1)
    cg_copy = pltpu.make_async_copy(cg, cg_out, out_sem.at[0])
    cg_copy.start()
    for layer in reversed(range(1, layers)):
        for rp in range(2):
            for copy in halos(layer, rp):
                copy.wait_recv()
        edges_then_inside(functools.partial(step, layer), layer - 1)

    def finish(q):
        for rp in range(2):
            last[rp, q - 1] = conv_at(0, rp, q).astype(BF16)

    def hid_copy(start, count, sem):
        part = pl.ds(start, count)
        return pltpu.make_async_copy(last.at[:, part], hid_out.at[:, part], out_sem.at[sem])

    pl.loop(2, quads)(finish)
    hid_copy(1, quads - 2, 1).start()
    for rp in range(2):
        for copy in halos(0, rp):
            copy.wait_recv()
    finish(1)
    hid_copy(0, 1, 2).start()
    finish(quads)
    hid_copy(quads - 1, 1, 3).start()

    @pl.loop(1, devices)
    def _(off):
        slots_to(lax.rem(me + off, devices)).wait_send()

    for layer in range(layers):
        for rp in range(2):
            for copy in halos(layer, rp):
                copy.wait_send()

    cg_copy.wait()
    hid_copy(1, quads - 2, 1).wait()
    hid_copy(0, 1, 2).wait()
    hid_copy(quads - 1, 1, 3).wait()


def encode_kernel(cg_in, hid_in, enc, out, cg, hid, slabs, done, in_sem, out_sem):
    pairs, levels, lons, tile_lat = done.shape
    pitch = odd(levels)

    def reads(pair):
        part = pl.ds(2 * pair, 2)
        return (
            pltpu.make_async_copy(cg_in.at[:, part], cg.at[:, part], in_sem.at[pair, 0]),
            pltpu.make_async_copy(hid_in.at[:, part], hid.at[:, part], in_sem.at[pair, 1]),
        )

    def write(pair):
        part = pl.ds(pl.multiple_of(lons * pair, lons), lons)
        return pltpu.make_async_copy(done.at[pair], out.at[:, part, :], out_sem.at[pair])

    @pl.loop(0, pairs)
    def _(pair):
        for copy in reads(pair):
            copy.start()

    @pl.loop(0, pairs)
    def _(pair):
        for copy in reads(pair):
            copy.wait()
        for half in range(2):
            for rp in range(2):
                q = 2 * pair + half
                state = cg[rp, q, 0:levels].astype(F32) + jnp.dot(
                    enc[...], hid[rp, q], preferred_element_type=F32
                )
                for r in range(2):
                    lon = half * 4 + rp * 2 + r
                    slabs[lon * pitch : lon * pitch + levels, :] = state[
                        :, r * tile_lat : (r + 1) * tile_lat
                    ]
        for level in range(levels):
            done[pair, level] = slabs[pl.ds(level, lons, stride=pitch), :]
        write(pair).start()

    @pl.loop(0, pairs)
    def _(pair):
        write(pair).wait()


def per_device(
    observation_residual, obs_index, obs_count, obs_weight, jacobian, decoder, conv_weight, gates, encoder
):
    lat_n, lon_n = lax.axis_size("lat"), lax.axis_size("lon")
    devices = lat_n * lon_n
    channels, slots = observation_residual.shape
    slot = slots // devices
    kinds_n, levels = jacobian.shape[1:]
    layers, width, tile_lon, tile_lat = gates.shape
    lev = up(levels + 2, 16)
    lanes = up(levels + 2, 128)
    quads = tile_lon // 4

    dims = (lat_n, lon_n, slot, kinds_n, levels, layers, width, tile_lon, tile_lat)
    vmem = pl.BlockSpec(memory_space=pltpu.VMEM)
    hbm = pl.BlockSpec(memory_space=pl.ANY)
    dma = pltpu.SemaphoreType.DMA
    cg_shape = (2, quads, lev, 2 * tile_lat)
    hid_shape = (2, quads, width, 2 * tile_lat)
    column_grad, hidden = pl.pallas_call(
        functools.partial(kernel, dims),
        out_shape=[
            jax.ShapeDtypeStruct(cg_shape, BF16),
            jax.ShapeDtypeStruct(hid_shape, BF16),
        ],
        in_specs=[vmem] * 7 + [hbm],
        out_specs=[hbm, hbm],
        scratch_shapes=[
            pltpu.VMEM((slots, lanes), BF16),
            pltpu.VMEM((slots, lanes), BF16),
            pltpu.VMEM((lev, slots), BF16),
            pltpu.VMEM((slots, tile_lat), BF16),
            pltpu.VMEM(cg_shape, BF16),
            pltpu.VMEM(hid_shape, F32),
            pltpu.VMEM(hid_shape, BF16),
            pltpu.VMEM((layers, 2, (quads + 2) * width, 2 * tile_lat), BF16),
            pltpu.VMEM((2, width, tile_lon, tile_lat), BF16),
            pltpu.VMEM((layers, up(width * odd(tile_lon), 8), tile_lat), F32),
            pltpu.VMEM((layers, width, 3 * width), BF16),
            pltpu.VMEM((width, lev), BF16),
            pltpu.VMEM((lanes, width), F32),
            pltpu.VMEM((lev * kinds_n, channels), F32),
            pltpu.VMEM((lev, kinds_n * channels), BF16),
            dma((devices,)),
            dma((devices,)),
            dma((layers, 2, 2)),
            dma((layers, 2, 2)),
            dma((2,)),
            dma((4,)),
        ],
        compiler_params=pltpu.CompilerParams(
            collective_id=0, has_side_effects=True, vmem_limit_bytes=60 * 1024 * 1024
        ),
    )(
        observation_residual, obs_index, obs_count, obs_weight.reshape(1, channels),
        jnp.transpose(jacobian, (2, 1, 0)), decoder, conv_weight, gates,
    )
    return pl.pallas_call(
        encode_kernel,
        out_shape=jax.ShapeDtypeStruct((levels, tile_lon, tile_lat), F32),
        in_specs=[hbm, hbm, vmem],
        out_specs=hbm,
        scratch_shapes=[
            pltpu.VMEM(cg_shape, BF16),
            pltpu.VMEM(hid_shape, BF16),
            pltpu.VMEM((up(8 * odd(levels), 8), tile_lat), F32),
            pltpu.VMEM((quads // 2, levels, 8, tile_lat), F32),
            dma((quads // 2, 2)),
            dma((quads // 2,)),
        ],
        compiler_params=pltpu.CompilerParams(vmem_limit_bytes=60 * 1024 * 1024),
    )(column_grad, hidden, jnp.transpose(encoder))


def solution(mesh):
    return jax.shard_map(
        per_device,
        mesh=mesh,
        in_specs=(
            P(None, ("lat", "lon")),
            P(None, ("lat", "lon")),
            P(None, ("lat", "lon")),
            P(),
            P(),
            P(),
            P(),
            P(None, None, "lon", "lat"),
            P(),
        ),
        out_specs=P(None, "lon", "lat"),
        check_vma=False,
    )
```
